32 devices in a mesh: sta: 8 (over z, y), tm: 4 (over x, core).
Axes of the slice: x: 2, y: 2, z: 4, core: 2. Of those that a mesh axis runs over, the one named last changes fastest.
Arguments:
- signal: bfloat16 [256, 12288], P('sta', 'tm'), may hold values from -6 to 6
- fir: float32 [4, 32], replicated, may hold values from -1 to 1
- taps: int32 [4], replicated, may hold values from 16 to 32, as said below
- sources: int32 [2, 16], replicated, may hold values from 0 to 255, as said below
Outputs:
- correlations: bfloat16 [2, 4, 16, 256, 512], P(None, None, None, 'sta', 'tm')
The draws below stay inside these ranges and needn't reach their ends.
Inputs may be any that keep to these rules, and one draw needn't show every extreme that they name: Each band has between 16 and 32 taps, and some band has exactly 32. `sources`: the source channels of one round are distinct.
All inputs are finite; a program needn't handle non-finite values.
Results may differ from the reference program's by a relative error of at most 0.0058.
Values may be sent and summed in bfloat16 or wider, within the bound.
A program may use at most 128 MiB of HBM per device.

```python
import jax
import jax.numpy as jnp
from jax import lax

SOURCES = 16
ROUNDS = 2
BANDS = 4
TAPS_MAX = 32
MAXLAG = 256
LAGS = 512
CHANNELS = 256
SAMPLES = 12288


def draw_taps(key, part):
    lower = jax.random.randint(key, (BANDS,), TAPS_MAX // 2, TAPS_MAX + 1)
    chosen = jax.random.randint(jax.random.fold_in(key, 7), (), 0, BANDS)
    return jnp.where(jnp.arange(BANDS) == chosen, TAPS_MAX, lower).astype(jnp.int32)


def draw_sources(key, part):
    round_keys = jax.random.split(key, ROUNDS)
    picked = jax.vmap(lambda single: jax.random.permutation(single, CHANNELS)[:SOURCES])(round_keys)
    return picked.astype(jnp.int32)


def block_scale(own_key, extent, cuts, smallest, largest):
    factor_of = 1.0
    for dim, shards_of in cuts:
        heights = jax.random.uniform(jax.random.fold_in(jax.random.fold_in(own_key, 6), dim), (shards_of,), jnp.float32, smallest / len(cuts), largest / len(cuts))
        factor_of = factor_of * jnp.repeat(jnp.exp(heights), extent[dim] // shards_of).reshape((-1,) + (1,) * (len(extent) - 1 - dim))
    return factor_of


def scatter_about(stream_key, shape, spread, most, shards=(), kind=jnp.bfloat16):
    result = jax.random.normal(stream_key, shape, jnp.float32) * spread
    if len(shards) > 0:
        result = block_scale(stream_key, shape, shards, -0.22, 0.18) * result
    return jnp.clip(result, min=-most, max=most).astype(kind)


def setup_inputs(seed: int = 0) -> dict:
    key_list = jax.random.split(jax.random.key(seed), 5)
    signal = scatter_about(key_list[0], (CHANNELS, SAMPLES), 1.0, 6.0, ((0, 8), (1, 4)))
    fir = scatter_about(key_list[1], (BANDS, TAPS_MAX), TAPS_MAX ** -0.5, 1.0, (), jnp.float32)
    taps = draw_taps(jax.random.fold_in(key_list[4], 71), 0)
    sources = draw_sources(jax.random.fold_in(key_list[4], 71), 0)
    return dict(signal=signal, fir=fir, taps=taps, sources=sources)


def skew(values, count_rows):
    leading = values.shape[:-1]
    length = values.shape[-1]
    row_width = length + count_rows
    padded = jnp.concatenate([values, jnp.zeros(leading + (count_rows,), values.dtype)], axis=-1)
    repeated = jnp.tile(padded, (1,) * len(leading) + (count_rows,))
    return repeated[..., : count_rows * (row_width - 1)].reshape(leading + (count_rows, row_width - 1))


def reference(signal, fir, taps, sources):
    active = jnp.arange(TAPS_MAX, dtype=jnp.int32)[None, :] < taps[:, None]
    coefficients = jnp.where(active, fir, 0.0).astype(jnp.bfloat16).astype(jnp.float32)
    traces = signal.astype(jnp.float32)
    padded = jnp.pad(traces, ((0, 0), (TAPS_MAX - 1, 0)))

    def one_band(weights):
        total = jnp.zeros(traces.shape, jnp.float32)
        for shift in range(TAPS_MAX):
            begin = TAPS_MAX - 1 - shift
            total = total + weights[shift] * padded[:, begin:begin + SAMPLES]
        return total.astype(jnp.bfloat16)

    filtered = lax.map(one_band, coefficients)
    norm_scale = SAMPLES ** -0.5
    rounds_out = []
    for rnd in range(ROUNDS):
        bands_out = []
        for band in range(BANDS):
            rows_band = filtered[band]
            picked = jnp.take(rows_band, sources[rnd], axis=0).astype(jnp.float32)
            hankel = skew(picked, LAGS)
            window = jnp.pad(rows_band, ((0, 0), (MAXLAG, MAXLAG)))[:, : SAMPLES + 2 * MAXLAG - 1].astype(jnp.float32)
            flat = hankel.reshape(SOURCES * LAGS, SAMPLES + 2 * MAXLAG - 1)
            product = jnp.dot(window, flat.T, preferred_element_type=jnp.float32) * norm_scale
            product = product.astype(jnp.bfloat16).reshape(CHANNELS, SOURCES, LAGS)
            bands_out.append(jnp.transpose(product, (1, 0, 2)))
        rounds_out.append(jnp.stack(bands_out, axis=0))
    return jnp.stack(rounds_out, axis=0)
```

```python
import functools

import jax
import jax.numpy as jnp
from jax import lax
from jax.experimental import pallas as pl
from jax.experimental.pallas import tpu as pltpu
from jax.sharding import PartitionSpec as P

ROUNDS = 2
MAXLAG = 256
LANES = 128
TILES = 8
CHUNK = 1792


def kernel(
    bands, sources, share, norm_scale,
    own_ref, src_ref, coef_ref, out_ref, raw, own_f, src_f, total,
):
    shards, channels, length = own_ref.shape
    samples = shards * length
    pad = own_f.shape[2] - samples - MAXLAG
    src_pad = src_f.shape[2] - samples - LANES
    rows = channels + sources

    raw[:, :LANES] = jnp.zeros((rows, LANES), raw.dtype)
    for shard in range(shards):
        at = pl.ds(LANES + shard * length, length)
        raw[:channels, at] = own_ref[shard]
        raw[channels:, at] = src_ref[shard]
    for band in range(bands):
        own_f[band, :, :MAXLAG] = jnp.zeros((channels, MAXLAG), own_f.dtype)
        own_f[band, :, pl.ds(MAXLAG + samples, pad)] = jnp.zeros((channels, pad), own_f.dtype)
        src_f[band, :, :LANES] = jnp.zeros((sources, LANES), src_f.dtype)
        src_f[band, :, pl.ds(LANES + samples, src_pad)] = jnp.zeros((sources, src_pad), src_f.dtype)

    weights = []
    for band in range(bands):
        base = jnp.broadcast_to(coef_ref[pl.ds(band, 1), :], (2 * LANES, 2 * LANES))
        turned = pltpu.roll(base, LANES, 1, stride=1, stride_axis=0)
        weights.append(turned[:, :LANES].astype(jnp.bfloat16))
    weights = jnp.concatenate(weights, axis=1)

    def filter_step(step, carry):
        begin = pl.multiple_of(step * (TILES * LANES), TILES * LANES)
        window = raw[:, pl.ds(begin, (TILES + 1) * LANES)]
        stacked = jnp.concatenate(
            [window[:, k * LANES : (k + 2) * LANES] for k in range(TILES)], axis=0
        )
        found = jnp.dot(stacked, weights, preferred_element_type=jnp.float32)
        found = found.astype(jnp.bfloat16)
        for k in range(TILES):
            for band in range(bands):
                part = found[k * rows : (k + 1) * rows, band * LANES : (band + 1) * LANES]
                own_f[band, :, pl.ds(MAXLAG + begin + k * LANES, LANES)] = part[:channels]
                src_f[band, :, pl.ds(LANES + begin + k * LANES, LANES)] = part[channels:]
        return carry

    lax.fori_loop(0, samples // (TILES * LANES), filter_step, 0)

    lag_base = lax.axis_index("tm") * share
    low = LANES // sources
    high = 4
    groups = sources // high
    chunks = (samples + LANES + CHUNK - 1) // CHUNK
    lane = lax.broadcasted_iota(jnp.int32, (16, LANES), 1)

    def band_step(band, carry):
        def chunk_step(chunk, carry):
            begin = pl.multiple_of(chunk * CHUNK, CHUNK)
            src_win = src_f[band, :, pl.ds(begin, CHUNK + LANES)]
            own_win = own_f[
                band, :, pl.ds(pl.multiple_of(begin + lag_base, LANES), CHUNK + LANES)
            ]
            left = jnp.concatenate(
                [own_win[:, high * g : high * g + CHUNK] for g in range(groups)], axis=0
            )
            right = []
            for q_high in range(high):
                for q_low in range(low):
                    shift = LANES - (sources * q_low + q_high)
                    right.append(src_win[:, shift : shift + CHUNK])
            right = jnp.concatenate(right, axis=0)
            term = lax.dot_general(
                left, right, (((1,), (1,)), ((), ())), preferred_element_type=jnp.float32
            )

            @pl.when(chunk == 0)
            def _():
                total[...] = term

            @pl.when(chunk > 0)
            def _():
                total[...] += term

            return carry

        lax.fori_loop(0, chunks, chunk_step, 0)

        for c in range(0, channels, 16):
            blocks = [
                total[g * channels + c : g * channels + c + 16, k * LANES : (k + 1) * LANES]
                for g in range(groups)
                for k in range(high)
            ]
            bit = 1
            while bit < sources:
                odd = (lane & bit) != 0
                for e in range(sources):
                    if e & bit == 0:
                        a, b = blocks[e], blocks[e | bit]
                        blocks[e] = jnp.where(odd, pltpu.roll(b, bit, 1), a)
                        blocks[e | bit] = jnp.where(odd, b, pltpu.roll(a, LANES - bit, 1))
                bit *= 2
            per_round = sources // ROUNDS
            for s in range(sources):
                out_ref[s // per_round, band, s % per_round, c : c + 16, :] = (
                    blocks[s] * norm_scale
                ).astype(out_ref.dtype)
        return carry

    lax.fori_loop(0, bands, band_step, 0)


def per_device(signal, fir, taps, sources):
    channels, length = signal.shape
    bands, tap_limit = fir.shape
    shards = lax.axis_size("tm")
    samples = length * shards
    share = 2 * MAXLAG // shards
    count = sources.size

    active = jnp.arange(tap_limit, dtype=jnp.int32)[None, :] < taps[:, None]
    coefficients = jnp.where(active, fir, 0.0).astype(jnp.bfloat16).astype(jnp.float32)
    coefficients = jnp.pad(coefficients, ((0, 0), (0, 2 * LANES - tap_limit)))

    local_ids = sources.reshape(-1) - lax.axis_index("sta") * channels
    onehot = (local_ids[:, None] == jnp.arange(channels, dtype=jnp.int32)[None, :]).astype(
        jnp.bfloat16
    )
    picked = jnp.dot(onehot, signal, preferred_element_type=jnp.float32).astype(jnp.bfloat16)
    picked = lax.psum(picked, "sta")
    own = lax.all_gather(signal, "tm")
    src = lax.all_gather(picked, "tm")

    chunks = (samples + LANES + CHUNK - 1) // CHUNK
    span = chunks * CHUNK
    return pl.pallas_call(
        functools.partial(kernel, bands, count, share, samples ** (-0.5)),
        out_shape=jax.ShapeDtypeStruct(
            (ROUNDS, bands, count // ROUNDS, channels, share), jnp.bfloat16
        ),
        in_specs=[pl.BlockSpec(memory_space=pltpu.VMEM)] * 3,
        out_specs=pl.BlockSpec(memory_space=pltpu.VMEM),
        scratch_shapes=[
            pltpu.VMEM((channels + count, LANES + samples), jnp.bfloat16),
            pltpu.VMEM((bands, channels, span + LANES + 2 * MAXLAG - share), jnp.bfloat16),
            pltpu.VMEM((bands, count, span + LANES), jnp.bfloat16),
            pltpu.VMEM((count // 4 * channels, 4 * LANES), jnp.float32),
        ],
        compiler_params=pltpu.CompilerParams(vmem_limit_bytes=52 * 2**20),
    )(own, src, coefficients)


def solution(mesh):
    in_specs = (P("sta", "tm"), P(), P(), P())
    out_specs = P(None, None, None, "sta", "tm")
    return jax.shard_map(
        per_device, mesh=mesh, in_specs=in_specs, out_specs=out_specs, check_vma=False
    )
```

```python
import functools

import jax
import jax.numpy as jnp
from jax import lax
from jax.experimental import pallas as pl
from jax.experimental.pallas import tpu as pltpu
from jax.sharding import PartitionSpec as P

ROUNDS = 2
MAXLAG = 256
LANES = 128
TILES = 8
MESH = pl.DeviceIdType.MESH
CHUNK = 1792


def kernel(
    bands, inner, norm_scale,
    signal_ref, ids_ref, coef_ref, out_ref,
    own_raw, src_raw, part, landed, across, raw, own_f, src_f, shifted, total,
    rs_send, rs_recv, out_send, out_recv, ag_send, ag_recv, x_send, x_recv,
    core_send, core_recv, own_send, own_recv,
):
    shards, channels, length = own_raw.shape
    sources = ids_ref.shape[0]
    outer = lax.axis_size("sta") // inner
    piece = length // inner
    samples = shards * length
    share = 2 * MAXLAG // shards
    pad = own_f.shape[2] - samples - MAXLAG
    src_pad = src_f.shape[2] - samples - LANES
    span = shifted.shape[2]

    sta, tm = lax.axis_index("sta"), lax.axis_index("tm")
    base, mine = (sta // inner) * inner, sta % inner
    far = (tm + shards // 2) % shards
    twin = tm + 1 - 2 * (tm % 2)
    far_twin = (twin + shards // 2) % shards

    def near(k):
        return base + (mine + k + inner) % inner

    def group(k):
        return (sta + k * inner + outer * inner) % (outer * inner)

    def send(src, dst, send_sem, recv_sem, device):
        return pltpu.make_async_remote_copy(
            src_ref=src, dst_ref=dst, send_sem=send_sem, recv_sem=recv_sem,
            device_id=device, device_id_type=MESH,
        )

    barrier = pltpu.get_barrier_semaphore()
    partners = [(near(k), tm) for k in range(1, inner)]
    partners += [(group(k), tm) for k in range(1, outer)]
    partners += [(sta, far), (sta, twin)]
    for partner in partners:
        pl.semaphore_signal(barrier, inc=1, device_id=partner, device_id_type=MESH)

    local = ids_ref[...] - sta * channels
    onehot = (
        local == lax.broadcasted_iota(jnp.int32, (sources, channels), 1)
    ).astype(jnp.float32).astype(jnp.bfloat16)
    own_raw[tm] = signal_ref[...]
    for j in range(inner):
        part[j] = jnp.dot(
            onehot, signal_ref[:, j * piece : (j + 1) * piece], preferred_element_type=jnp.float32
        ).astype(jnp.bfloat16)

    pl.semaphore_wait(barrier, len(partners))

    scatter = []
    for k in range(1, inner):
        to = (mine + k) % inner
        copy = send(part.at[to], landed.at[k], rs_send.at[k], rs_recv.at[k], (near(k), tm))
        copy.start()
        scatter.append(copy)
    own_far = send(own_raw.at[tm], own_raw.at[tm], own_send.at[0], own_recv.at[0], (sta, far))
    own_far.start()
    own_twin = send(own_raw.at[tm], own_raw.at[tm], own_send.at[1], own_recv.at[1], (sta, twin))
    own_twin.start()

    raw[:, :LANES] = jnp.zeros((raw.shape[0], LANES), raw.dtype)
    for band in range(bands):
        own_f[band, :, :MAXLAG] = jnp.zeros((channels, MAXLAG), own_f.dtype)
        own_f[band, :, pl.ds(MAXLAG + samples, pad)] = jnp.zeros((channels, pad), own_f.dtype)
        src_f[band, :, :LANES] = jnp.zeros((sources, LANES), src_f.dtype)
        src_f[band, :, pl.ds(LANES + samples, src_pad)] = jnp.zeros((sources, src_pad), src_f.dtype)

    weights = []
    for band in range(bands):
        row = jnp.broadcast_to(coef_ref[pl.ds(band, 1), :], (2 * LANES, 2 * LANES))
        turned = pltpu.roll(row, LANES, 1, stride=1, stride_axis=0)
        weights.append(turned[:, :LANES].astype(jnp.bfloat16))
    weights = jnp.concatenate(weights, axis=1)

    summed = part[mine].astype(jnp.float32)
    for k in range(1, inner):
        scatter[k - 1].wait_recv()
        summed += landed[k].astype(jnp.float32)
    if outer > 1:
        across[0] = summed.astype(jnp.bfloat16)
        exchange = []
        for k in range(1, outer):
            copy = send(
                across.at[0], across.at[k], out_send.at[k], out_recv.at[k], (group(k), tm)
            )
            copy.start()
            exchange.append(copy)
        for copy in exchange:
            copy.wait_recv()
        for k in range(1, outer):
            summed += across[k].astype(jnp.float32)
        for copy in exchange:
            copy.wait_send()
    src_raw[tm, mine] = summed.astype(jnp.bfloat16)

    own_slot = src_raw.at[tm, mine]
    gather = []
    for k in range(1, inner):
        copy = send(own_slot, own_slot, ag_send.at[k], ag_recv.at[k], (near(k), tm))
        copy.start()
        gather.append(copy)
    along = [send(own_slot, own_slot, x_send.at[0], x_recv.at[0], (sta, far))]
    along[0].start()

    own_from_far = send(
        own_raw.at[far], own_raw.at[far], own_send.at[2], own_recv.at[0], (sta, twin)
    )
    own_from_far.wait_recv()
    own_pass = send(own_raw.at[far], own_raw.at[far], own_send.at[2], own_recv.at[2], (sta, twin))
    own_pass.start()

    def arrived(k):
        slot = src_raw.at[tm, (mine - k + inner) % inner]
        send(slot, slot, ag_send.at[k], ag_recv.at[k], (near(k), tm)).wait_recv()
        copy = send(slot, slot, x_send.at[k], x_recv.at[k], (sta, far))
        copy.start()
        along.append(copy)

    for k in range(1, inner):
        arrived(k)
    row_twin = send(src_raw.at[tm], src_raw.at[tm], core_send.at[0], core_recv.at[0], (sta, twin))
    row_twin.start()

    own_twin.wait_recv()
    own_pass.wait_recv()
    for shard in range(shards):
        raw[:channels, pl.ds(LANES + shard * length, length)] = own_raw[shard]

    def filtered(first, rows, target, offset):
        def filter_step(step, carry):
            begin = pl.multiple_of(step * (TILES * LANES), TILES * LANES)
            window = raw[first : first + rows, pl.ds(begin, (TILES + 1) * LANES)]
            stacked = jnp.concatenate(
                [window[:, k * LANES : (k + 2) * LANES] for k in range(TILES)], axis=0
            )
            found = jnp.dot(stacked, weights, preferred_element_type=jnp.float32)
            found = found.astype(jnp.bfloat16)
            for k in range(TILES):
                for band in range(bands):
                    target[band, :, pl.ds(offset + begin + k * LANES, LANES)] = found[
                        k * rows : (k + 1) * rows, band * LANES : (band + 1) * LANES
                    ]
            return carry

        lax.fori_loop(0, samples // (TILES * LANES), filter_step, 0)

    low = LANES // sources
    high = 4
    groups = sources // high
    chunks = span // CHUNK
    lag_base = tm * share

    filtered(0, channels, own_f, MAXLAG)

    for k in range(inner):
        slot = src_raw.at[far, (mine - k + inner) % inner]
        send(slot, slot, x_send.at[k], x_recv.at[k], (sta, far)).wait_recv()
    far_pass = send(src_raw.at[far], src_raw.at[far], core_send.at[1], core_recv.at[1], (sta, twin))
    far_pass.start()

    def shift_band(band, carry):
        def shift_step(chunk, carry):
            begin = pl.multiple_of(chunk * CHUNK, CHUNK)
            window = own_f[
                band, :, pl.ds(pl.multiple_of(begin + lag_base, LANES), CHUNK + LANES)
            ]
            for g in range(groups):
                shifted[band, pl.ds(g * channels, channels), pl.ds(begin, CHUNK)] = window[
                    :, high * g : high * g + CHUNK
                ]
            return carry

        return lax.fori_loop(0, chunks, shift_step, carry)

    lax.fori_loop(0, bands, shift_band, 0)

    for source, index in ((twin, 0), (far_twin, 1)):
        slot = src_raw.at[source]
        send(slot, slot, core_send.at[index], core_recv.at[index], (sta, twin)).wait_recv()
    for shard in range(shards):
        for j in range(inner):
            raw[channels:, pl.ds(LANES + shard * length + j * piece, piece)] = src_raw[shard, j]
    for copy in scatter + gather + along + [own_far, own_twin, own_pass, row_twin, far_pass]:
        copy.wait_send()

    filtered(channels, sources, src_f, LANES)

    lane = lax.broadcasted_iota(jnp.int32, (16, LANES), 1)

    def band_step(band, carry):
        def chunk_step(chunk, carry):
            begin = pl.multiple_of(chunk * CHUNK, CHUNK)
            src_win = src_f[band, :, pl.ds(begin, CHUNK + LANES)]
            left = shifted[band, :, pl.ds(begin, CHUNK)]
            right = []
            for q_high in range(high):
                for q_low in range(low):
                    shift = LANES - (sources * q_low + q_high)
                    right.append(src_win[:, shift : shift + CHUNK])
            right = jnp.concatenate(right, axis=0)
            term = lax.dot_general(
                left, right, (((1,), (1,)), ((), ())), preferred_element_type=jnp.float32
            )

            @pl.when(chunk == 0)
            def _():
                total[...] = term

            @pl.when(chunk > 0)
            def _():
                total[...] += term

            return carry

        lax.fori_loop(0, chunks, chunk_step, 0)

        for c in range(0, channels, 16):
            blocks = [
                total[g * channels + c : g * channels + c + 16, k * LANES : (k + 1) * LANES]
                for g in range(groups)
                for k in range(high)
            ]
            bit = 1
            while bit < sources:
                odd = (lane & bit) != 0
                for e in range(sources):
                    if e & bit == 0:
                        a, b = blocks[e], blocks[e | bit]
                        blocks[e] = jnp.where(odd, pltpu.roll(b, bit, 1), a)
                        blocks[e | bit] = jnp.where(odd, b, pltpu.roll(a, LANES - bit, 1))
                bit *= 2
            per_round = sources // ROUNDS
            for s in range(sources):
                out_ref[s // per_round, band, s % per_round, c : c + 16, :] = (
                    blocks[s] * norm_scale
                ).astype(out_ref.dtype)
        return carry

    lax.fori_loop(0, bands, band_step, 0)


def per_device(signal, fir, taps, sources):
    channels, length = signal.shape
    bands, tap_limit = fir.shape
    shards, stations = lax.axis_size("tm"), lax.axis_size("sta")
    samples = length * shards
    share = 2 * MAXLAG // shards
    count = sources.size
    inner = max(
        d for d in range(1, stations + 1) if stations % d == 0 and length % (d * LANES) == 0
    )
    outer = stations // inner
    piece = length // inner

    active = jnp.arange(tap_limit, dtype=jnp.int32)[None, :] < taps[:, None]
    coefficients = jnp.where(active, fir, 0.0).astype(jnp.bfloat16).astype(jnp.float32)
    coefficients = jnp.pad(coefficients, ((0, 0), (0, 2 * LANES - tap_limit)))

    chunks = (samples + LANES + CHUNK - 1) // CHUNK
    span = chunks * CHUNK
    groups = count // 4
    dma = pltpu.SemaphoreType.DMA
    return pl.pallas_call(
        functools.partial(kernel, bands, inner, samples ** (-0.5)),
        out_shape=jax.ShapeDtypeStruct(
            (ROUNDS, bands, count // ROUNDS, channels, share), jnp.bfloat16
        ),
        in_specs=[pl.BlockSpec(memory_space=pltpu.VMEM)] * 3,
        out_specs=pl.BlockSpec(memory_space=pltpu.VMEM),
        scratch_shapes=[
            pltpu.VMEM((shards, channels, length), jnp.bfloat16),
            pltpu.VMEM((shards, inner, count, piece), jnp.bfloat16),
            pltpu.VMEM((inner, count, piece), jnp.bfloat16),
            pltpu.VMEM((inner, count, piece), jnp.bfloat16),
            pltpu.VMEM((outer, count, piece), jnp.bfloat16),
            pltpu.VMEM((channels + count, LANES + samples), jnp.bfloat16),
            pltpu.VMEM((bands, channels, span + LANES + 2 * MAXLAG - share), jnp.bfloat16),
            pltpu.VMEM((bands, count, span + LANES), jnp.bfloat16),
            pltpu.VMEM((bands, groups * channels, span), jnp.bfloat16),
            pltpu.VMEM((groups * channels, 4 * LANES), jnp.float32),
            dma((inner,)), dma((inner,)), dma((outer,)), dma((outer,)),
            dma((inner,)), dma((inner,)), dma((inner,)), dma((inner,)),
            dma((2,)), dma((2,)), dma((3,)), dma((3,)),
        ],
        compiler_params=pltpu.CompilerParams(
            vmem_limit_bytes=58 * 2**20, collective_id=0, has_side_effects=True
        ),
    )(signal, sources.reshape(count, 1), coefficients)


def solution(mesh):
    in_specs = (P("sta", "tm"), P(), P(), P())
    out_specs = P(None, None, None, "sta", "tm")
    return jax.shard_map(
        per_device, mesh=mesh, in_specs=in_specs, out_specs=out_specs, check_vma=False
    )
```

```python
import functools

import jax
import jax.numpy as jnp
from jax import lax
from jax.experimental import pallas as pl
from jax.experimental.pallas import tpu as pltpu
from jax.sharding import PartitionSpec as P

ROUNDS = 2
MAXLAG = 256
LANES = 128
TILES = 8
MESH = pl.DeviceIdType.MESH
CHUNK = 12544


def kernel(
    bands, inner, norm_scale,
    signal_ref, ids_ref, coef_ref, out_ref,
    own_raw, src_raw, part, landed, across, raw, own_f, src_f, shifted, total,
    rs_send, rs_recv, out_send, out_recv, ag_send, ag_recv, x_send, x_recv,
    core_send, core_recv, own_send, own_recv,
):
    shards, channels, length = own_raw.shape
    sources = ids_ref.shape[0]
    outer = lax.axis_size("sta") // inner
    piece = length // inner
    samples = shards * length
    share = 2 * MAXLAG // shards
    pad = own_f.shape[2] - samples - MAXLAG
    src_pad = src_f.shape[2] - samples - LANES
    span = shifted.shape[2]

    sta, tm = lax.axis_index("sta"), lax.axis_index("tm")
    base, mine = (sta // inner) * inner, sta % inner
    far = (tm + shards // 2) % shards
    twin = tm + 1 - 2 * (tm % 2)
    far_twin = (twin + shards // 2) % shards

    def near(k):
        return base + (mine + k + inner) % inner

    def group(k):
        return (sta + k * inner + outer * inner) % (outer * inner)

    def send(src, dst, send_sem, recv_sem, device):
        return pltpu.make_async_remote_copy(
            src_ref=src, dst_ref=dst, send_sem=send_sem, recv_sem=recv_sem,
            device_id=device, device_id_type=MESH,
        )

    barrier = pltpu.get_barrier_semaphore()
    partners = [(near(k), tm) for k in range(1, inner)]
    partners += [(group(k), tm) for k in range(1, outer)]
    partners += [(sta, far), (sta, twin)]
    for partner in partners:
        pl.semaphore_signal(barrier, inc=1, device_id=partner, device_id_type=MESH)

    local = ids_ref[...] - sta * channels
    onehot = (
        local == lax.broadcasted_iota(jnp.int32, (sources, channels), 1)
    ).astype(jnp.float32).astype(jnp.bfloat16)
    own_raw[tm] = signal_ref[...]
    for j in range(inner):
        part[j] = jnp.dot(
            onehot, signal_ref[:, j * piece : (j + 1) * piece], preferred_element_type=jnp.float32
        ).astype(jnp.bfloat16)

    pl.semaphore_wait(barrier, len(partners))

    scatter = []
    for k in range(1, inner):
        to = (mine + k) % inner
        copy = send(part.at[to], landed.at[k], rs_send.at[k], rs_recv.at[k], (near(k), tm))
        copy.start()
        scatter.append(copy)
    own_far = send(own_raw.at[tm], own_raw.at[tm], own_send.at[0], own_recv.at[0], (sta, far))
    own_far.start()
    own_twin = send(own_raw.at[tm], own_raw.at[tm], own_send.at[1], own_recv.at[1], (sta, twin))
    own_twin.start()

    raw[:, :LANES] = jnp.zeros((raw.shape[0], LANES), raw.dtype)
    for band in range(bands):
        own_f[band, :, :MAXLAG] = jnp.zeros((channels, MAXLAG), own_f.dtype)
        own_f[band, :, pl.ds(MAXLAG + samples, pad)] = jnp.zeros((channels, pad), own_f.dtype)
        src_f[band, :, :LANES] = jnp.zeros((sources, LANES), src_f.dtype)
        src_f[band, :, pl.ds(LANES + samples, src_pad)] = jnp.zeros((sources, src_pad), src_f.dtype)

    weights = []
    for band in range(bands):
        row = jnp.broadcast_to(coef_ref[pl.ds(band, 1), :], (2 * LANES, 2 * LANES))
        turned = pltpu.roll(row, LANES, 1, stride=1, stride_axis=0)
        weights.append(turned[:, :LANES].astype(jnp.bfloat16))
    weights = jnp.concatenate(weights, axis=1)

    summed = part[mine].astype(jnp.float32)
    for k in range(1, inner):
        scatter[k - 1].wait_recv()
        summed += landed[k].astype(jnp.float32)
    if outer > 1:
        across[0] = summed.astype(jnp.bfloat16)
        exchange = []
        for k in range(1, outer):
            copy = send(
                across.at[0], across.at[k], out_send.at[k], out_recv.at[k], (group(k), tm)
            )
            copy.start()
            exchange.append(copy)
        for copy in exchange:
            copy.wait_recv()
        for k in range(1, outer):
            summed += across[k].astype(jnp.float32)
        for copy in exchange:
            copy.wait_send()
    src_raw[tm, mine] = summed.astype(jnp.bfloat16)

    own_slot = src_raw.at[tm, mine]
    gather = []
    for k in range(1, inner):
        copy = send(own_slot, own_slot, ag_send.at[k], ag_recv.at[k], (near(k), tm))
        copy.start()
        gather.append(copy)
    along = [send(own_slot, own_slot, x_send.at[0], x_recv.at[0], (sta, far))]
    along[0].start()

    own_from_far = send(
        own_raw.at[far], own_raw.at[far], own_send.at[2], own_recv.at[0], (sta, twin)
    )
    own_from_far.wait_recv()
    own_pass = send(own_raw.at[far], own_raw.at[far], own_send.at[2], own_recv.at[2], (sta, twin))
    own_pass.start()

    def arrived(k):
        slot = src_raw.at[tm, (mine - k + inner) % inner]
        send(slot, slot, ag_send.at[k], ag_recv.at[k], (near(k), tm)).wait_recv()
        copy = send(slot, slot, x_send.at[k], x_recv.at[k], (sta, far))
        copy.start()
        along.append(copy)

    own_twin.wait_recv()
    own_pass.wait_recv()
    for shard in range(shards):
        raw[:channels, pl.ds(LANES + shard * length, length)] = own_raw[shard]

    def filtered(first, rows, target, offset):
        def filter_step(step, carry):
            begin = pl.multiple_of(step * (TILES * LANES), TILES * LANES)
            window = raw[first : first + rows, pl.ds(begin, (TILES + 1) * LANES)]
            stacked = jnp.concatenate(
                [window[:, k * LANES : (k + 2) * LANES] for k in range(TILES)], axis=0
            )
            found = jnp.dot(stacked, weights, preferred_element_type=jnp.float32)
            found = found.astype(jnp.bfloat16)
            for k in range(TILES):
                for band in range(bands):
                    target[band, :, pl.ds(offset + begin + k * LANES, LANES)] = found[
                        k * rows : (k + 1) * rows, band * LANES : (band + 1) * LANES
                    ]
            return carry

        lax.fori_loop(0, samples // (TILES * LANES), filter_step, 0)

    low = LANES // sources
    high = 4
    groups = sources // high
    chunks = span // CHUNK
    lag_base = tm * share


    def shift_band(band, carry):
        def shift_step(chunk, carry):
            begin = pl.multiple_of(chunk * CHUNK, LANES)
            window = own_f[
                band, :, pl.ds(pl.multiple_of(begin + lag_base, LANES), CHUNK + LANES)
            ]
            for g in range(groups):
                shifted[band, pl.ds(g * channels, channels), pl.ds(begin, CHUNK)] = window[
                    :, high * g : high * g + CHUNK
                ]
            return carry

        return lax.fori_loop(0, chunks, shift_step, carry)

    filtered(0, channels, own_f, MAXLAG)
    early = 1
    lax.fori_loop(0, early, shift_band, 0)
    for k in range(1, inner):
        arrived(k)
    row_twin = send(src_raw.at[tm], src_raw.at[tm], core_send.at[0], core_recv.at[0], (sta, twin))
    row_twin.start()

    lax.fori_loop(early, bands, shift_band, 0)
    for k in range(inner):
        slot = src_raw.at[far, (mine - k + inner) % inner]
        send(slot, slot, x_send.at[k], x_recv.at[k], (sta, far)).wait_recv()
    far_pass = send(src_raw.at[far], src_raw.at[far], core_send.at[1], core_recv.at[1], (sta, twin))
    far_pass.start()


    for source, index in ((twin, 0), (far_twin, 1)):
        slot = src_raw.at[source]
        send(slot, slot, core_send.at[index], core_recv.at[index], (sta, twin)).wait_recv()
    for shard in range(shards):
        for j in range(inner):
            raw[channels:, pl.ds(LANES + shard * length + j * piece, piece)] = src_raw[shard, j]
    for copy in scatter + gather + along + [own_far, own_twin, own_pass, row_twin, far_pass]:
        copy.wait_send()

    filtered(channels, sources, src_f, LANES)

    lane = lax.broadcasted_iota(jnp.int32, (16, LANES), 1)

    def band_step(band, carry):
        def chunk_step(chunk, carry):
            begin = pl.multiple_of(chunk * CHUNK, LANES)
            src_win = src_f[band, :, pl.ds(begin, CHUNK + LANES)]
            left = shifted[band, :, pl.ds(begin, CHUNK)]
            right = []
            for q_high in range(high):
                for q_low in range(low):
                    shift = LANES - (sources * q_low + q_high)
                    right.append(src_win[:, shift : shift + CHUNK])
            right = jnp.concatenate(right, axis=0)
            term = lax.dot_general(
                left, right, (((1,), (1,)), ((), ())), preferred_element_type=jnp.float32
            )

            @pl.when(chunk == 0)
            def _():
                total[...] = term

            @pl.when(chunk > 0)
            def _():
                total[...] += term

            return carry

        lax.fori_loop(0, chunks, chunk_step, 0)

        for c in range(0, channels, 16):
            blocks = [
                total[g * channels + c : g * channels + c + 16, k * LANES : (k + 1) * LANES]
                for g in range(groups)
                for k in range(high)
            ]
            bit = 1
            while bit < sources:
                odd = (lane & bit) != 0
                for e in range(sources):
                    if e & bit == 0:
                        a, b = blocks[e], blocks[e | bit]
                        blocks[e] = jnp.where(odd, pltpu.roll(b, bit, 1), a)
                        blocks[e | bit] = jnp.where(odd, b, pltpu.roll(a, LANES - bit, 1))
                bit *= 2
            per_round = sources // ROUNDS
            for s in range(sources):
                out_ref[s // per_round, band, s % per_round, c : c + 16, :] = (
                    blocks[s] * norm_scale
                ).astype(out_ref.dtype)
        return carry

    lax.fori_loop(0, bands, band_step, 0)


def per_device(signal, fir, taps, sources):
    channels, length = signal.shape
    bands, tap_limit = fir.shape
    shards, stations = lax.axis_size("tm"), lax.axis_size("sta")
    samples = length * shards
    share = 2 * MAXLAG // shards
    count = sources.size
    inner = max(
        d for d in range(1, stations + 1) if stations % d == 0 and length % (d * LANES) == 0
    )
    outer = stations // inner
    piece = length // inner

    active = jnp.arange(tap_limit, dtype=jnp.int32)[None, :] < taps[:, None]
    coefficients = jnp.where(active, fir, 0.0).astype(jnp.bfloat16).astype(jnp.float32)
    coefficients = jnp.pad(coefficients, ((0, 0), (0, 2 * LANES - tap_limit)))

    chunks = (samples + LANES + CHUNK - 1) // CHUNK
    span = chunks * CHUNK
    groups = count // 4
    dma = pltpu.SemaphoreType.DMA
    return pl.pallas_call(
        functools.partial(kernel, bands, inner, samples ** (-0.5)),
        out_shape=jax.ShapeDtypeStruct(
            (ROUNDS, bands, count // ROUNDS, channels, share), jnp.bfloat16
        ),
        in_specs=[pl.BlockSpec(memory_space=pltpu.VMEM)] * 3,
        out_specs=pl.BlockSpec(memory_space=pltpu.VMEM),
        scratch_shapes=[
            pltpu.VMEM((shards, channels, length), jnp.bfloat16),
            pltpu.VMEM((shards, inner, count, piece), jnp.bfloat16),
            pltpu.VMEM((inner, count, piece), jnp.bfloat16),
            pltpu.VMEM((inner, count, piece), jnp.bfloat16),
            pltpu.VMEM((outer, count, piece), jnp.bfloat16),
            pltpu.VMEM((channels + count, LANES + samples), jnp.bfloat16),
            pltpu.VMEM((bands, channels, span + LANES + 2 * MAXLAG - share), jnp.bfloat16),
            pltpu.VMEM((bands, count, span + LANES), jnp.bfloat16),
            pltpu.VMEM((bands, groups * channels, span), jnp.bfloat16),
            pltpu.VMEM((groups * channels, 4 * LANES), jnp.float32),
            dma((inner,)), dma((inner,)), dma((outer,)), dma((outer,)),
            dma((inner,)), dma((inner,)), dma((inner,)), dma((inner,)),
            dma((2,)), dma((2,)), dma((3,)), dma((3,)),
        ],
        compiler_params=pltpu.CompilerParams(
            vmem_limit_bytes=58 * 2**20, collective_id=0, has_side_effects=True
        ),
    )(signal, sources.reshape(count, 1), coefficients)


def solution(mesh):
    in_specs = (P("sta", "tm"), P(), P(), P())
    out_specs = P(None, None, None, "sta", "tm")
    return jax.shard_map(
        per_device, mesh=mesh, in_specs=in_specs, out_specs=out_specs, check_vma=False
    )
```

```python
import functools

import jax
import jax.numpy as jnp
from jax import lax
from jax.experimental import pallas as pl
from jax.experimental.pallas import tpu as pltpu
from jax.sharding import PartitionSpec as P

ROUNDS = 2
MAXLAG = 256
LANES = 128
TILES = 8
MESH = pl.DeviceIdType.MESH
CHUNK = 12544


def kernel(
    bands, inner, norm_scale,
    signal_ref, fir_ref, taps_ref, ids_ref, out_ref,
    own_raw, src_raw, part, landed, across, raw, own_f, src_f, shifted, total, coef_ref,
    rs_send, rs_recv, out_send, out_recv, ag_send, ag_recv, x_send, x_recv,
    core_send, core_recv, own_send, own_recv,
):
    shards, channels, length = own_raw.shape
    rounds, per_round = ids_ref.shape
    sources = rounds * per_round
    tap_limit = fir_ref.shape[1]
    outer = lax.axis_size("sta") // inner
    piece = length // inner
    samples = shards * length
    share = 2 * MAXLAG // shards
    pad = own_f.shape[2] - samples - MAXLAG
    src_pad = src_f.shape[2] - samples - LANES
    span = shifted.shape[2]

    sta, tm = lax.axis_index("sta"), lax.axis_index("tm")
    base, mine = (sta // inner) * inner, sta % inner
    far = (tm + shards // 2) % shards
    twin = tm + 1 - 2 * (tm % 2)
    far_twin = (twin + shards // 2) % shards

    def near(k):
        return base + (mine + k + inner) % inner

    def group(k):
        return (sta + k * inner + outer * inner) % (outer * inner)

    def send(src, dst, send_sem, recv_sem, device):
        return pltpu.make_async_remote_copy(
            src_ref=src, dst_ref=dst, send_sem=send_sem, recv_sem=recv_sem,
            device_id=device, device_id_type=MESH,
        )

    barrier = pltpu.get_barrier_semaphore()
    partners = [(near(k), tm) for k in range(1, inner)]
    partners += [(group(k), tm) for k in range(1, outer)]
    partners += [(sta, far), (sta, twin)]
    for partner in partners:
        pl.semaphore_signal(barrier, inc=1, device_id=partner, device_id_type=MESH)

    at_row = lax.broadcasted_iota(jnp.int32, (sources, channels), 0)
    ids = jnp.zeros((sources, channels), jnp.int32)
    for s in range(sources):
        ids = jnp.where(at_row == s, ids_ref[s // per_round, s % per_round], ids)
    local = ids - sta * channels
    onehot = (
        local == lax.broadcasted_iota(jnp.int32, (sources, channels), 1)
    ).astype(jnp.float32).astype(jnp.bfloat16)
    own_raw[tm] = signal_ref[...]
    for j in range(inner):
        part[j] = jnp.dot(
            onehot, signal_ref[:, j * piece : (j + 1) * piece], preferred_element_type=jnp.float32
        ).astype(jnp.bfloat16)

    pl.semaphore_wait(barrier, len(partners))

    scatter = []
    for k in range(1, inner):
        to = (mine + k) % inner
        copy = send(part.at[to], landed.at[k], rs_send.at[k], rs_recv.at[k], (near(k), tm))
        copy.start()
        scatter.append(copy)
    own_far = send(own_raw.at[tm], own_raw.at[tm], own_send.at[0], own_recv.at[0], (sta, far))
    own_far.start()
    own_twin = send(own_raw.at[tm], own_raw.at[tm], own_send.at[1], own_recv.at[1], (sta, twin))
    own_twin.start()

    raw[:, :LANES] = jnp.zeros((raw.shape[0], LANES), raw.dtype)
    for band in range(bands):
        own_f[band, :, :MAXLAG] = jnp.zeros((channels, MAXLAG), own_f.dtype)
        own_f[band, :, pl.ds(MAXLAG + samples, pad)] = jnp.zeros((channels, pad), own_f.dtype)
        src_f[band, :, :LANES] = jnp.zeros((sources, LANES), src_f.dtype)
        src_f[band, :, pl.ds(LANES + samples, src_pad)] = jnp.zeros((sources, src_pad), src_f.dtype)

    coef_ref[...] = jnp.zeros_like(coef_ref)
    tap = lax.broadcasted_iota(jnp.int32, (1, tap_limit), 1)
    for band in range(bands):
        coef_ref[band : band + 1, :tap_limit] = jnp.where(
            tap < taps_ref[band], fir_ref[band : band + 1, :], 0.0
        )
    weights = []
    for band in range(bands):
        row = jnp.broadcast_to(coef_ref[pl.ds(band, 1), :], (2 * LANES, 2 * LANES))
        turned = pltpu.roll(row, LANES, 1, stride=1, stride_axis=0)
        weights.append(turned[:, :LANES].astype(jnp.bfloat16))
    weights = jnp.concatenate(weights, axis=1)

    summed = part[mine].astype(jnp.float32)
    for k in range(1, inner):
        scatter[k - 1].wait_recv()
        summed += landed[k].astype(jnp.float32)
    if outer > 1:
        across[0] = summed.astype(jnp.bfloat16)
        exchange = []
        for k in range(1, outer):
            copy = send(
                across.at[0], across.at[k], out_send.at[k], out_recv.at[k], (group(k), tm)
            )
            copy.start()
            exchange.append(copy)
        for copy in exchange:
            copy.wait_recv()
        for k in range(1, outer):
            summed += across[k].astype(jnp.float32)
        for copy in exchange:
            copy.wait_send()
    src_raw[tm, mine] = summed.astype(jnp.bfloat16)

    own_slot = src_raw.at[tm, mine]
    gather = []
    for k in range(1, inner):
        copy = send(own_slot, own_slot, ag_send.at[k], ag_recv.at[k], (near(k), tm))
        copy.start()
        gather.append(copy)
    along = [send(own_slot, own_slot, x_send.at[0], x_recv.at[0], (sta, far))]
    along[0].start()

    own_from_far = send(
        own_raw.at[far], own_raw.at[far], own_send.at[2], own_recv.at[0], (sta, twin)
    )
    own_from_far.wait_recv()
    own_pass = send(own_raw.at[far], own_raw.at[far], own_send.at[2], own_recv.at[2], (sta, twin))
    own_pass.start()

    def arrived(k):
        slot = src_raw.at[tm, (mine - k + inner) % inner]
        send(slot, slot, ag_send.at[k], ag_recv.at[k], (near(k), tm)).wait_recv()
        copy = send(slot, slot, x_send.at[k], x_recv.at[k], (sta, far))
        copy.start()
        along.append(copy)

    own_twin.wait_recv()
    own_pass.wait_recv()
    for shard in range(shards):
        raw[:channels, pl.ds(LANES + shard * length, length)] = own_raw[shard]

    def filtered(first, rows, target, offset):
        def filter_step(step, carry):
            begin = pl.multiple_of(step * (TILES * LANES), TILES * LANES)
            window = raw[first : first + rows, pl.ds(begin, (TILES + 1) * LANES)]
            stacked = jnp.concatenate(
                [window[:, k * LANES : (k + 2) * LANES] for k in range(TILES)], axis=0
            )
            found = jnp.dot(stacked, weights, preferred_element_type=jnp.float32)
            found = found.astype(jnp.bfloat16)
            for k in range(TILES):
                for band in range(bands):
                    target[band, :, pl.ds(offset + begin + k * LANES, LANES)] = found[
                        k * rows : (k + 1) * rows, band * LANES : (band + 1) * LANES
                    ]
            return carry

        lax.fori_loop(0, samples // (TILES * LANES), filter_step, 0)

    low = LANES // sources
    high = 4
    groups = sources // high
    chunks = span // CHUNK
    lag_base = tm * share


    def shift_band(band, carry):
        def shift_step(chunk, carry):
            begin = pl.multiple_of(chunk * CHUNK, LANES)
            window = own_f[
                band, :, pl.ds(pl.multiple_of(begin + lag_base, LANES), CHUNK + LANES)
            ]
            for g in range(groups):
                shifted[band, pl.ds(g * channels, channels), pl.ds(begin, CHUNK)] = window[
                    :, high * g : high * g + CHUNK
                ]
            return carry

        return lax.fori_loop(0, chunks, shift_step, carry)

    filtered(0, channels, own_f, MAXLAG)
    early = 0
    lax.fori_loop(0, early, shift_band, 0)
    for k in range(1, inner):
        arrived(k)
    row_twin = send(src_raw.at[tm], src_raw.at[tm], core_send.at[0], core_recv.at[0], (sta, twin))
    row_twin.start()

    lax.fori_loop(early, bands, shift_band, 0)
    for k in range(inner):
        slot = src_raw.at[far, (mine - k + inner) % inner]
        send(slot, slot, x_send.at[k], x_recv.at[k], (sta, far)).wait_recv()
    far_pass = send(src_raw.at[far], src_raw.at[far], core_send.at[1], core_recv.at[1], (sta, twin))
    far_pass.start()


    for source, index in ((twin, 0), (far_twin, 1)):
        slot = src_raw.at[source]
        send(slot, slot, core_send.at[index], core_recv.at[index], (sta, twin)).wait_recv()
    for shard in range(shards):
        for j in range(inner):
            raw[channels:, pl.ds(LANES + shard * length + j * piece, piece)] = src_raw[shard, j]
    for copy in scatter + gather + along + [own_far, own_twin, own_pass, row_twin, far_pass]:
        copy.wait_send()

    filtered(channels, sources, src_f, LANES)

    lane = lax.broadcasted_iota(jnp.int32, (16, LANES), 1)

    def band_step(band, carry):
        def chunk_step(chunk, carry):
            begin = pl.multiple_of(chunk * CHUNK, LANES)
            src_win = src_f[band, :, pl.ds(begin, CHUNK + LANES)]
            left = shifted[band, :, pl.ds(begin, CHUNK)]
            right = []
            for q_high in range(high):
                for q_low in range(low):
                    shift = LANES - (sources * q_low + q_high)
                    right.append(src_win[:, shift : shift + CHUNK])
            right = jnp.concatenate(right, axis=0)
            term = lax.dot_general(
                left, right, (((1,), (1,)), ((), ())), preferred_element_type=jnp.float32
            )

            total[...] = term

            return carry

        lax.fori_loop(0, chunks, chunk_step, 0)

        for c in range(0, channels, 16):
            blocks = [
                total[g * channels + c : g * channels + c + 16, k * LANES : (k + 1) * LANES]
                for g in range(groups)
                for k in range(high)
            ]
            bit = 1
            while bit < sources:
                odd = (lane & bit) != 0
                for e in range(sources):
                    if e & bit == 0:
                        a, b = blocks[e], blocks[e | bit]
                        blocks[e] = jnp.where(odd, pltpu.roll(b, bit, 1), a)
                        blocks[e | bit] = jnp.where(odd, b, pltpu.roll(a, LANES - bit, 1))
                bit *= 2
            for s in range(sources):
                out_ref[s // per_round, band, s % per_round, c : c + 16, :] = (
                    blocks[s] * norm_scale
                ).astype(out_ref.dtype)
        return carry

    lax.fori_loop(0, bands, band_step, 0)


def per_device(signal, fir, taps, sources):
    channels, length = signal.shape
    bands = fir.shape[0]
    shards, stations = lax.axis_size("tm"), lax.axis_size("sta")
    samples = length * shards
    share = 2 * MAXLAG // shards
    count = sources.size
    inner = max(
        d for d in range(1, stations + 1) if stations % d == 0 and length % (d * LANES) == 0
    )
    outer = stations // inner
    piece = length // inner

    chunks = (samples + LANES + CHUNK - 1) // CHUNK
    span = chunks * CHUNK
    assert chunks == 1
    groups = count // 4
    dma = pltpu.SemaphoreType.DMA
    return pl.pallas_call(
        functools.partial(kernel, bands, inner, samples ** (-0.5)),
        out_shape=jax.ShapeDtypeStruct(
            (ROUNDS, bands, count // ROUNDS, channels, share), jnp.bfloat16
        ),
        in_specs=[pl.BlockSpec(memory_space=pltpu.VMEM)] * 2
        + [pl.BlockSpec(memory_space=pltpu.SMEM)] * 2,
        out_specs=pl.BlockSpec(memory_space=pltpu.VMEM),
        scratch_shapes=[
            pltpu.VMEM((shards, channels, length), jnp.bfloat16),
            pltpu.VMEM((shards, inner, count, piece), jnp.bfloat16),
            pltpu.VMEM((inner, count, piece), jnp.bfloat16),
            pltpu.VMEM((inner, count, piece), jnp.bfloat16),
            pltpu.VMEM((outer, count, piece), jnp.bfloat16),
            pltpu.VMEM((channels + count, LANES + samples), jnp.bfloat16),
            pltpu.VMEM((bands, channels, span + LANES + 2 * MAXLAG - share), jnp.bfloat16),
            pltpu.VMEM((bands, count, span + LANES), jnp.bfloat16),
            pltpu.VMEM((bands, groups * channels, span), jnp.bfloat16),
            pltpu.VMEM((groups * channels, 4 * LANES), jnp.float32),
            pltpu.VMEM((bands, 2 * LANES), jnp.float32),
            dma((inner,)), dma((inner,)), dma((outer,)), dma((outer,)),
            dma((inner,)), dma((inner,)), dma((inner,)), dma((inner,)),
            dma((2,)), dma((2,)), dma((3,)), dma((3,)),
        ],
        compiler_params=pltpu.CompilerParams(
            vmem_limit_bytes=58 * 2**20, collective_id=0, has_side_effects=True
        ),
    )(signal, fir, taps, sources)


def solution(mesh):
    in_specs = (P("sta", "tm"), P(), P(), P())
    out_specs = P(None, None, None, "sta", "tm")
    return jax.shard_map(
        per_device, mesh=mesh, in_specs=in_specs, out_specs=out_specs, check_vma=False
    )
```
